32 devices in a mesh: slide: 2 (over x), row: 8 (over z, y), col: 2 (over core).
Axes of the slice: x: 2, y: 2, z: 4, core: 2. Of those that a mesh axis runs over, the one named last changes fastest.
Arguments:
- features: bfloat16 [32768, 1024], P(('slide', 'row', 'col')), parts along dimension 0, may hold values from -6 to 6
- seq_order: int32 [32, 1024], P(('slide', 'row', 'col')), parts along dimension 0, may hold values from 0 to 1023, each once within a row
- block_links: int32 [9, 32, 8], P(None, ('slide', 'row'), 'col'), parts along dimension 1, may hold values 0 or 1
- start_vectors: float32 [32, 32, 1024], P(None, ('slide', 'row'), 'col'), parts along dimension 1, may hold values from -6 to 6
Outputs:
- eigen_fields: float32 [32, 32, 1024], P(None, ('slide', 'row'), 'col'), parts along dimension 1
The draws below stay inside these ranges and needn't reach their ends.
There are 2 independent parts, one for each index of `slide`. The reference program is written for one: setup_inputs(seed, part) draws one part's arguments, and reference() takes and returns one part's arrays. A program takes and returns all parts, laid end to end along the dimension named above; each array names one. Nothing has to cross between parts.
Inputs may be any that keep to these rules, and one draw needn't show every extreme that they name: Each row of seq_order lists every number of 0 to 1023 once. `block_links`: entries of the centre offset 4 are not read.
All inputs are finite; a program needn't handle non-finite values. No bound on the sum of `block_links` on one device may be relied on, other than what follows from the above.
Results may differ from the reference program's by a relative error of at most 0.0021.
Values may be sent and summed in bfloat16 or wider, within the bound.
A program may use at most 64 MiB of HBM per device.

```python
import jax
import jax.numpy as jnp
from jax import lax

D = 1024
K = 32
BLK = 128
CAND = 9
ITERS = 3
TH = 2
NBL = 4
TOK_DEV = 1024
H = 16
NBW = 8
W = 1024
SHARDS = 16
TOKENS = 16384
N_ROW = 8
N_COL = 2


def place_ends(array, key, low, top_value):
    longest = array.shape.index(max(array.shape))
    spots = []
    for shift in (0, 1):
        where = [jax.random.randint(jax.random.fold_in(key, axis), (), 0, length) for axis, length in enumerate(array.shape)]
        where[longest] = (where[longest] + shift) % array.shape[longest]
        spots.append(tuple(where))
    return array.at[spots[0]].set(low).at[spots[1]].set(top_value)


def shard_levels(key, shape, shards, least, top_value):
    gain = 1.0
    for axis_at, parts in shards:
        steps = jax.random.uniform(jax.random.fold_in(jax.random.fold_in(key, 6), axis_at), (parts,), jnp.float32, least / len(shards), top_value / len(shards))
        gain = gain * jnp.repeat(jnp.exp(steps), shape[axis_at] // parts).reshape((-1,) + (1,) * (len(shape) - 1 - axis_at))
    return gain


def noise(rng, extent, spread, reach, shards=(), held_as=jnp.bfloat16):
    array = spread * jax.random.normal(rng, extent, jnp.float32)
    if shards:
        array = array * shard_levels(rng, extent, shards, -0.22, 0.18)
    return jnp.clip(array, -reach, reach).astype(held_as)


def setup_inputs(seed: int = 0, part: int = 0) -> dict:
    streams_of = jax.random.split(jax.random.key(seed), 5)
    part_keys = jax.random.split(jax.random.fold_in(streams_of[4], part), 5)
    features = noise(part_keys[0], (TOKENS, D), 1.0, 6.0, ((0, 16),))
    seq_order = jax.vmap(lambda own: jax.random.permutation(own, TOK_DEV))(jax.random.split(part_keys[1], SHARDS)).reshape((SHARDS, TOK_DEV)).astype(jnp.int32)
    block_links = place_ends((jax.random.randint(part_keys[2], (CAND, H, NBW), 0, 2) < 1).astype(jnp.int32), jax.random.fold_in(part_keys[2], 1), 0, 1)
    start_vectors = noise(part_keys[3], (K, H, W), 1.0, 6.0, ((1, 8), (2, 2)), jnp.float32)
    return dict(features=features, seq_order=seq_order, block_links=block_links, start_vectors=start_vectors)


SHARPNESS = 4.0
EPSILON = 1e-06

def reference(features, seq_order, block_links, start_vectors):
    height = TH * N_ROW
    blocks_w = NBL * N_COL
    strip_w = NBL * BLK // N_ROW
    wide = features.astype(jnp.float32)
    unit_rows = (wide * lax.rsqrt(lax.optimization_barrier(jnp.sum(wide * wide, axis=1, keepdims=True)) + EPSILON)).astype(jnp.bfloat16)
    strips = unit_rows.reshape(N_ROW * N_COL, TOK_DEV, D)
    placed = jax.vmap(lambda piece, where: piece[where])(strips, seq_order)
    image = placed.reshape(N_ROW, N_COL, height, strip_w, D).transpose(2, 1, 0, 3, 4)
    image = image.reshape(height, blocks_w, BLK, D)
    padded = jnp.pad(image, ((1, 1), (1, 1), (0, 0), (0, 0)))
    row_pos = jnp.arange(height)
    col_pos = jnp.arange(blocks_w)
    link_list = []
    for offset in range(9):
        step_row = offset // 3 - 1
        step_col = offset % 3 - 1
        inside = ((row_pos + step_row >= 0) & (row_pos + step_row < height))[:, None] & ((col_pos + step_col >= 0) & (col_pos + step_col < blocks_w))[None, :]
        chosen = inside if offset == 4 else inside & (block_links[offset] == 1)
        link_list.append(chosen.astype(jnp.float32))
    link_rows = jnp.stack(link_list).transpose(1, 0, 2)

    def row_tiles(inputs):
        row_index, link_row = inputs
        near = lax.dynamic_slice_in_dim(padded, row_index, 3, 0)
        center = near[1, 1:blocks_w + 1].astype(jnp.float32)
        result = []
        for offset in range(9):
            step_row = offset // 3 - 1
            step_col = offset % 3 - 1
            shifted = near[step_row + 1, 1 + step_col:1 + step_col + blocks_w].astype(jnp.float32)
            dots = jnp.einsum('xid,xjd->xij', center, shifted)
            result.append(jnp.exp(SHARPNESS * (dots - 1.0)) * link_row[offset][:, None, None])
        return jnp.stack(result)
    tiles = lax.map(row_tiles, (jnp.arange(height).astype(jnp.int32), link_rows))
    degree = lax.optimization_barrier(jnp.sum(tiles, axis=(1, 4)))

    def propagate(field):
        rimmed = jnp.pad(field, ((0, 0), (1, 1), (1, 1), (0, 0)))
        total = jnp.zeros_like(field)
        for offset in range(9):
            step_row = offset // 3 - 1
            step_col = offset % 3 - 1
            shifted = rimmed[:, 1 + step_row:1 + step_row + height, 1 + step_col:1 + step_col + blocks_w]
            total = total + jnp.einsum('yxij,kyxj->kyxi', tiles[:, offset], shifted, precision=lax.Precision.HIGHEST)
        return total / degree
    vectors = start_vectors.reshape(K, height, blocks_w, BLK)
    for step in range(ITERS):
        grown = propagate(vectors)
        flat = grown.reshape(K, -1)
        gram = jnp.dot(flat, flat.T, precision=lax.Precision.HIGHEST)
        lower_factor = jnp.linalg.cholesky(gram)
        vectors = jax.scipy.linalg.solve_triangular(lower_factor, flat, lower=True).reshape(grown.shape)
    scale = float(TOKENS) ** 0.5
    return vectors.reshape(K, height, blocks_w * BLK) * scale
```

```python
import functools
import math

import jax
import jax.numpy as jnp
from jax import lax
from jax.experimental import pallas as pl
from jax.experimental.pallas import tpu as pltpu
from jax.sharding import PartitionSpec as P

ITERS = 3
SHARPNESS = 4.0
EPSILON = 1e-06
HIGHEST = lax.Precision.HIGHEST
F32 = jnp.float32
BF16 = jnp.bfloat16
LANES = 128
STEPS = ((-1, 0), (1, 0), (0, -1), (0, 1), (-1, -1), (-1, 1), (1, -1), (1, 1))


def whiten(gram):
    k = gram.shape[0]
    rows = lax.broadcasted_iota(jnp.int32, (k, k), 0)
    cols = lax.broadcasted_iota(jnp.int32, (k, k), 1)
    eye = (rows == cols).astype(F32)
    work = jnp.concatenate([gram, eye], axis=1)
    at = lax.broadcasted_iota(jnp.int32, (k, 1), 0)
    for step in range(k - 1):
        pivot = work[step : step + 1, :]
        pivot = pivot / pivot[:, step : step + 1]
        below = jnp.where(at > step, work[:, step : step + 1], 0.0)
        work = work - below * pivot
    diag = jnp.sum(work[:, :k] * eye, axis=1, keepdims=True)
    return work[:, k:] / jnp.sqrt(diag)


def kernel(
    rows_n, cols_n, th, nb, sw, scale,
    feat_ref, seq_ref, link_ref, start_ref, out_ref,
    unit, placed, land, fpad, thi, tlo, deg, vpad, grown, gsend, grecv,
    a2a_send, a2a_recv, halo_send, halo_recv, gram_send, gram_recv,
):
    row, col = lax.axis_index("row"), lax.axis_index("col")
    peers = rows_n * cols_n
    me = row * cols_n + col
    tokens, width = feat_ref.shape
    vec_n = start_ref.shape[0]
    bw = LANES
    blocks = th * nb
    chunk = th * sw
    per = LANES // chunk
    supers = tokens // LANES

    def at(peer):
        return {"row": peer // cols_n, "col": lax.rem(peer, cols_n)}

    def exists(dr, dc):
        r, c = row + dr, col + dc
        return (r >= 0) & (r < rows_n) & (c >= 0) & (c < cols_n)

    def piece(buf, dr, dc, arriving):
        def pick(step, n):
            if step == 0:
                return pl.ds(1, n)
            if arriving:
                return pl.ds(n + 1 if step < 0 else 0, 1)
            return pl.ds(1 if step < 0 else n, 1)

        return buf.at[pick(dr, th), pick(dc, nb)]

    def halo_copy(buf, stage, way, sending):
        dr, dc = STEPS[way]
        r = row + dr if sending else row - dr
        c = col + dc if sending else col - dc
        return pltpu.make_async_remote_copy(
            src_ref=piece(buf, dr, dc, False),
            dst_ref=piece(buf, dr, dc, True),
            send_sem=halo_send.at[stage, way],
            recv_sem=halo_recv.at[stage, way],
            device_id={"row": r, "col": c},
            device_id_type=pl.DeviceIdType.MESH,
        )

    def halo_start(buf, stage):
        for way, (dr, dc) in enumerate(STEPS):
            @pl.when(exists(dr, dc))
            def _():
                halo_copy(buf, stage, way, True).start()

    def halo_wait(buf, stage, ways=range(8)):
        for way in ways:
            dr, dc = STEPS[way]

            @pl.when(exists(-dr, -dc))
            def _():
                halo_copy(buf, stage, way, False).wait_recv()

    def halo_finish(buf, stage):
        for way, (dr, dc) in enumerate(STEPS):
            @pl.when(exists(dr, dc))
            def _():
                halo_copy(buf, stage, way, True).wait_send()

    def halo_zero(buf):
        for dr, dc in STEPS:
            @pl.when(jnp.logical_not(exists(-dr, -dc)))
            def _():
                where = piece(buf, dr, dc, True)
                where[...] = jnp.zeros(where.shape, where.dtype)

    barrier = pltpu.get_barrier_semaphore()

    @pl.loop(1, peers)
    def _(step):
        pl.semaphore_signal(
            barrier, inc=1, device_id=at(lax.rem(me + step, peers)),
            device_id_type=pl.DeviceIdType.MESH,
        )

    for y in range(th):
        for x in range(nb):
            lo = (y * nb + x) * bw
            vpad[0, 1 + y, 1 + x] = start_ref[:, lo : lo + bw]
    for step in range(ITERS):
        halo_zero(vpad.at[step])
    halo_zero(fpad)
    deg[...] = jnp.zeros_like(deg)

    @pl.loop(0, tokens // 64)
    def _(step):
        rows = pl.ds(pl.multiple_of(step * 64, 64), 64)
        wide = feat_ref[rows, :].astype(F32)
        squares = jnp.sum(wide * wide, axis=1, keepdims=True)
        unit[rows, :] = (wide * lax.rsqrt(squares + EPSILON)).astype(BF16)

    pl.semaphore_wait(barrier, peers - 1)
    halo_start(vpad.at[0], 0)

    def strip_copy(index, part, dest, source):
        return pltpu.make_async_remote_copy(
            src_ref=placed.at[index, pl.ds(part * chunk, chunk)],
            dst_ref=land.at[source],
            send_sem=a2a_send.at[dest],
            recv_sem=a2a_recv.at[source],
            device_id={"row": dest},
            device_id_type=pl.DeviceIdType.MESH,
        )

    @pl.loop(0, supers)
    def _(step):
        index = lax.rem(row // per + 1 + step, supers)
        order = seq_ref[:, pl.ds(pl.multiple_of(index * LANES, LANES), LANES)]
        order = jnp.broadcast_to(order.astype(F32), (LANES, LANES)).T
        lane = lax.broadcasted_iota(jnp.int32, (LANES, LANES), 1).astype(F32)
        chosen = jnp.concatenate(
            [
                jnp.where(order == lane + float(j * LANES), 1.0, 0.0).astype(BF16)
                for j in range(supers)
            ],
            axis=1,
        )
        placed[index] = jnp.dot(chosen, unit[...], preferred_element_type=F32).astype(BF16)
        for part in range(per):
            dest = index * per + part

            @pl.when(dest != row)
            def _():
                strip_copy(index, part, dest, row).start()

            @pl.when(dest == row)
            def _():
                land[dest] = placed[index, pl.ds(part * chunk, chunk)]

    group = max(1, 16 // sw)
    span = group * sw
    in_block = bw // span

    @pl.loop(0, rows_n // group)
    def _(step):
        first = lax.rem(row // group + step, rows_n // group)
        for i in range(group):
            source = first * group + i

            @pl.when(source != row)
            def _():
                strip_copy(0, 0, row, source).wait_recv()

        rows = pl.ds(pl.multiple_of(lax.rem(first, in_block) * span, span), span)
        x = 1 + first // in_block
        if group == 1:
            for y in range(th):
                fpad[1 + y, x, rows, :] = land[first, y * sw : (y + 1) * sw, :]
        else:
            wide = [land[first * group + i].astype(F32) for i in range(group)]
            for y in range(th):
                joined = jnp.concatenate([w[y * sw : (y + 1) * sw] for w in wide], axis=0)
                fpad[1 + y, x, rows, :] = joined.astype(BF16)

    halo_start(fpad, ITERS)

    def tile(y, x, dy, dx):
        offset = (dy + 1) * 3 + dx + 1
        block = y * nb + x
        near = fpad[1 + y + dy, 1 + x + dx]
        own = fpad[1 + y, 1 + x]
        dots = lax.dot_general(
            near, own, (((1,), (1,)), ((), ())), preferred_element_type=F32
        )
        at_row, at_col = row * th + y + dy, col * nb + x + dx
        inside = (at_row >= 0) & (at_row < rows_n * th)
        inside &= (at_col >= 0) & (at_col < cols_n * nb)
        if offset != 4:
            inside &= link_ref[offset * blocks + block] == 1
        link = jnp.where(inside, 1.0, 0.0).astype(F32)
        value = jnp.exp(SHARPNESS * (dots - 1.0)) * link
        deg[block] += jnp.sum(value, axis=0, keepdims=True)
        high = value.astype(BF16)
        thi[block, offset * bw : (offset + 1) * bw, :] = high
        tlo[block, offset * bw : (offset + 1) * bw, :] = (value - high.astype(F32)).astype(BF16)

    def tiles(y, dy):
        @pl.loop(0, nb)
        def _(x):
            tile(y, x, dy, 0)

        @pl.loop(1, nb)
        def _(x):
            tile(y, x, dy, -1)
            tile(y, x - 1, dy, 1)

    def side_tiles(y, dy):
        tile(y, 0, dy, -1)
        tile(y, nb - 1, dy, 1)

    inner = [(y, dy) for y in range(th) for dy in (-1, 0, 1) if 0 <= y + dy < th]
    for y, dy in inner:
        tiles(y, dy)
    halo_wait(fpad, ITERS, (2, 3))
    for y, dy in inner:
        side_tiles(y, dy)
    for edge, ways in (((0, -1), (1, 6, 7)), ((th - 1, 1), (0, 4, 5))):
        halo_wait(fpad, ITERS, ways)
        tiles(*edge)
        side_tiles(*edge)
    deg[...] = 1.0 / deg[...]

    def gram_copy(stage, dest, source):
        return pltpu.make_async_remote_copy(
            src_ref=gsend.at[stage],
            dst_ref=grecv.at[stage, source],
            send_sem=gram_send.at[stage, dest],
            recv_sem=gram_recv.at[stage, source],
            device_id=at(dest),
            device_id_type=pl.DeviceIdType.MESH,
        )

    pack = LANES // vec_n
    part_rows = vec_n // pack
    inverse = None
    for step in range(ITERS):
        halo_wait(vpad.at[step], step)

        @pl.loop(0, blocks)
        def _(block):
            y, x = block // nb, lax.rem(block, nb)
            field = jnp.concatenate(
                [vpad[step, y + o // 3, x + o % 3] for o in range(9)], axis=1
            )
            high = field.astype(BF16)
            low = (field - high.astype(F32)).astype(BF16)
            both = jnp.dot(
                jnp.concatenate([high, low], axis=0), thi[block], preferred_element_type=F32
            )
            total = both[:vec_n] + both[vec_n:]
            total += jnp.dot(high, tlo[block], preferred_element_type=F32)
            grown[:, pl.ds(pl.multiple_of(block * bw, bw), bw)] = total * deg[block]

        value = grown[...]
        if step:
            total = jnp.zeros((part_rows, LANES), F32)
            last = step - 1

            def add(source, total):
                @pl.when(source != me)
                def _():
                    gram_copy(last, me, source).wait_recv()

                return total + grecv[last, source]

            total = lax.fori_loop(0, peers, add, total)
            gram = jnp.concatenate(
                [total[:, i * vec_n : (i + 1) * vec_n] for i in range(pack)], axis=0
            )
            inverse = whiten(gram)
            value = jnp.dot(inverse, value, precision=HIGHEST, preferred_element_type=F32)
            grown[...] = value
        if step + 1 < ITERS:
            for y in range(th):
                for x in range(nb):
                    lo = (y * nb + x) * bw
                    vpad[step + 1, 1 + y, 1 + x] = value[:, lo : lo + bw]
            halo_start(vpad.at[step + 1], step + 1)
        gram = lax.dot_general(
            value, value, (((1,), (1,)), ((), ())),
            precision=HIGHEST, preferred_element_type=F32,
        )
        packed = jnp.concatenate(
            [gram[i * part_rows : (i + 1) * part_rows] for i in range(pack)], axis=1
        )
        gsend[step] = packed
        grecv[step, me] = packed

        @pl.loop(1, peers)
        def _(other):
            gram_copy(step, lax.rem(me + other, peers), me).start()

    def add(source, total):
        @pl.when(source != me)
        def _():
            gram_copy(ITERS - 1, me, source).wait_recv()

        return total + grecv[ITERS - 1, source]

    total = lax.fori_loop(0, peers, add, jnp.zeros((part_rows, LANES), F32))
    gram = jnp.concatenate(
        [total[:, i * vec_n : (i + 1) * vec_n] for i in range(pack)], axis=0
    )
    out_ref[...] = jnp.dot(
        whiten(gram), grown[...], precision=HIGHEST, preferred_element_type=F32
    ) * scale

    for step in range(ITERS):
        halo_finish(vpad.at[step], step)

        @pl.loop(1, peers)
        def _(other):
            gram_copy(step, lax.rem(me + other, peers), me).wait_send()

    halo_finish(fpad, ITERS)

    @pl.loop(0, rows_n)
    def _(dest):
        @pl.when(dest != row)
        def _():
            strip_copy(0, 0, dest, row).wait_send()


def body(features, seq_order, block_links, start_vectors):
    rows_n = lax.axis_size("row")
    cols_n = lax.axis_size("col")
    tokens, width = features.shape
    vec_n, th, tile_w = start_vectors.shape
    nb = block_links.shape[2]
    sw = tile_w // rows_n
    bw = tile_w // nb
    peers = rows_n * cols_n
    blocks = th * nb
    scale = math.sqrt(th * rows_n * tile_w * cols_n)
    part_rows = vec_n * vec_n // LANES
    vmem = pl.BlockSpec(memory_space=pltpu.VMEM)
    dma = pltpu.SemaphoreType.DMA
    out = pl.pallas_call(
        functools.partial(kernel, rows_n, cols_n, th, nb, sw, scale),
        out_shape=jax.ShapeDtypeStruct((vec_n, tokens), F32),
        in_specs=[vmem, vmem, pl.BlockSpec(memory_space=pltpu.SMEM), vmem],
        out_specs=vmem,
        scratch_shapes=[
            pltpu.VMEM((tokens, width), BF16),
            pltpu.VMEM((tokens // LANES, LANES, width), BF16),
            pltpu.VMEM((rows_n, th * sw, width), BF16),
            pltpu.VMEM((th + 2, nb + 2, bw, width), BF16),
            pltpu.VMEM((blocks, 9 * bw, bw), BF16),
            pltpu.VMEM((blocks, 9 * bw, bw), BF16),
            pltpu.VMEM((blocks, 1, bw), F32),
            pltpu.VMEM((ITERS, th + 2, nb + 2, vec_n, bw), F32),
            pltpu.VMEM((vec_n, tokens), F32),
            pltpu.VMEM((ITERS, part_rows, LANES), F32),
            pltpu.VMEM((ITERS, peers, part_rows, LANES), F32),
            dma((rows_n,)),
            dma((rows_n,)),
            dma((ITERS + 1, len(STEPS))),
            dma((ITERS + 1, len(STEPS))),
            dma((ITERS, peers)),
            dma((ITERS, peers)),
        ],
        compiler_params=pltpu.CompilerParams(
            collective_id=0, has_side_effects=True, vmem_limit_bytes=48 * 2**20
        ),
    )(features, seq_order, block_links.reshape(-1), start_vectors.reshape(vec_n, tokens))
    return out.reshape(vec_n, th, tile_w)


def solution(mesh):
    return jax.shard_map(
        body,
        mesh=mesh,
        in_specs=(
            P(("slide", "row", "col"), None),
            P(("slide", "row", "col"), None),
            P(None, ("slide", "row"), "col"),
            P(None, ("slide", "row"), "col"),
        ),
        out_specs=P(None, ("slide", "row"), "col"),
        check_vma=False,
    )
```

```python
import functools
import math

import jax
import jax.numpy as jnp
from jax import lax
from jax.experimental import pallas as pl
from jax.experimental.pallas import tpu as pltpu
from jax.sharding import PartitionSpec as P

ITERS = 3
SHARPNESS = 4.0
EPSILON = 1e-06
HIGHEST = lax.Precision.HIGHEST
F32 = jnp.float32
BF16 = jnp.bfloat16
LANES = 128
STEPS = ((-1, 0), (1, 0), (0, -1), (0, 1), (-1, -1), (-1, 1), (1, -1), (1, 1))


def snake(place, rows_n):
    if rows_n % 4:
        return place
    odd_pair = lax.rem(place // 2, 2)
    return place + odd_pair * (1 - 2 * lax.rem(place, 2))


def whiten(gram):
    k = gram.shape[0]
    rows = lax.broadcasted_iota(jnp.int32, (k, k), 0)
    cols = lax.broadcasted_iota(jnp.int32, (k, k), 1)
    eye = (rows == cols).astype(F32)
    work = jnp.concatenate([gram, eye], axis=1)
    at = lax.broadcasted_iota(jnp.int32, (k, 1), 0)
    for step in range(k - 1):
        pivot = work[step : step + 1, :]
        pivot = pivot / pivot[:, step : step + 1]
        below = jnp.where(at > step, work[:, step : step + 1], 0.0)
        work = work - below * pivot
    diag = jnp.sum(work[:, :k] * eye, axis=1, keepdims=True)
    return work[:, k:] / jnp.sqrt(diag)


def kernel(
    rows_n, cols_n, th, nb, sw, scale,
    feat_ref, seq_ref, link_ref, start_ref, out_ref,
    unit, placed, land, fpad, thi, tlo, deg, vpad, grown, gsend, grecv,
    begun, linked, swapped,
    a2a_send, a2a_recv, halo_send, halo_recv, gram_send, gram_recv, swap_send, swap_recv,
):
    row, col = lax.axis_index("row"), lax.axis_index("col")
    peers = rows_n * cols_n
    me = row * cols_n + col
    trow = snake(row, rows_n)
    moved = trow != row
    tokens, width = feat_ref.shape
    vec_n = start_ref.shape[0]
    bw = LANES
    blocks = th * nb
    chunk = th * sw
    per = LANES // chunk
    supers = tokens // LANES

    def at(peer):
        return {"row": peer // cols_n, "col": lax.rem(peer, cols_n)}

    def exists(dr, dc):
        r, c = trow + dr, col + dc
        return (r >= 0) & (r < rows_n) & (c >= 0) & (c < cols_n)

    def piece(buf, dr, dc, arriving):
        def pick(step, n):
            if step == 0:
                return pl.ds(1, n)
            if arriving:
                return pl.ds(n + 1 if step < 0 else 0, 1)
            return pl.ds(1 if step < 0 else n, 1)

        return buf.at[pick(dr, th), pick(dc, nb)]

    def halo_copy(buf, stage, way, sending):
        dr, dc = STEPS[way]
        r = snake(trow + dr if sending else trow - dr, rows_n)
        c = col + dc if sending else col - dc
        return pltpu.make_async_remote_copy(
            src_ref=piece(buf, dr, dc, False),
            dst_ref=piece(buf, dr, dc, True),
            send_sem=halo_send.at[stage, way],
            recv_sem=halo_recv.at[stage, way],
            device_id={"row": r, "col": c},
            device_id_type=pl.DeviceIdType.MESH,
        )

    def halo_start(buf, stage, ways=range(8)):
        for way in ways:
            dr, dc = STEPS[way]

            @pl.when(exists(dr, dc))
            def _():
                halo_copy(buf, stage, way, True).start()

    def halo_wait(buf, stage, ways=range(8)):
        for way in ways:
            dr, dc = STEPS[way]

            @pl.when(exists(-dr, -dc))
            def _():
                halo_copy(buf, stage, way, False).wait_recv()

    def halo_finish(buf, stage, ways=range(8)):
        for way in ways:
            dr, dc = STEPS[way]

            @pl.when(exists(dr, dc))
            def _():
                halo_copy(buf, stage, way, True).wait_send()

    def corner_copy(way):
        dr, dc = STEPS[way]
        edge = pl.ds(th + 1 if dr < 0 else 0, 1)
        return pltpu.make_async_remote_copy(
            src_ref=fpad.at[edge, pl.ds(1 if dc < 0 else nb, 1)],
            dst_ref=fpad.at[edge, pl.ds(nb + 1 if dc < 0 else 0, 1)],
            send_sem=halo_send.at[ITERS, way],
            recv_sem=halo_recv.at[ITERS, way],
            device_id={"col": col + dc},
            device_id_type=pl.DeviceIdType.MESH,
        )

    def corner_when(way, action):
        dr, dc = STEPS[way]

        @pl.when(exists(-dr, dc))
        def _():
            action(corner_copy(way))

    def swap_copy(src, dst, index):
        return pltpu.make_async_remote_copy(
            src_ref=src,
            dst_ref=dst,
            send_sem=swap_send.at[index],
            recv_sem=swap_recv.at[index],
            device_id={"row": trow},
            device_id_type=pl.DeviceIdType.MESH,
        )

    swaps = (
        (start_ref, begun, 0),
        (link_ref, linked, 1),
        (grown, swapped, 2),
    )

    def halo_zero(buf):
        for dr, dc in STEPS:
            @pl.when(jnp.logical_not(exists(-dr, -dc)))
            def _():
                where = piece(buf, dr, dc, True)
                where[...] = jnp.zeros(where.shape, where.dtype)

    barrier = pltpu.get_barrier_semaphore()

    @pl.loop(1, peers)
    def _(step):
        pl.semaphore_signal(
            barrier, inc=1, device_id=at(lax.rem(me + step, peers)),
            device_id_type=pl.DeviceIdType.MESH,
        )

    for step in range(ITERS):
        halo_zero(vpad.at[step])
    halo_zero(fpad)
    deg[...] = jnp.zeros_like(deg)

    @pl.loop(0, tokens // 64)
    def _(step):
        rows = pl.ds(pl.multiple_of(step * 64, 64), 64)
        wide = feat_ref[rows, :].astype(F32)
        squares = jnp.sum(wide * wide, axis=1, keepdims=True)
        unit[rows, :] = (wide * lax.rsqrt(squares + EPSILON)).astype(BF16)

    pl.semaphore_wait(barrier, peers - 1)

    @pl.when(moved)
    def _():
        for swap in swaps[:2]:
            swap_copy(*swap).start()

    @pl.when(jnp.logical_not(moved))
    def _():
        begun[...] = start_ref[...]
        linked[...] = link_ref[...]

    def strip_copy(index, part, dest, source):
        return pltpu.make_async_remote_copy(
            src_ref=placed.at[index, pl.ds(part * chunk, chunk)],
            dst_ref=land.at[source],
            send_sem=a2a_send.at[dest],
            recv_sem=a2a_recv.at[source],
            device_id={"row": snake(dest, rows_n)},
            device_id_type=pl.DeviceIdType.MESH,
        )

    @pl.loop(0, supers)
    def _(step):
        index = lax.rem(trow // per + 1 + step, supers)
        order = seq_ref[:, pl.ds(pl.multiple_of(index * LANES, LANES), LANES)]
        order = jnp.broadcast_to(order.astype(F32), (LANES, LANES)).T
        lane = lax.broadcasted_iota(jnp.int32, (LANES, LANES), 1).astype(F32)
        chosen = jnp.concatenate(
            [
                jnp.where(order == lane + float(j * LANES), 1.0, 0.0).astype(BF16)
                for j in range(supers)
            ],
            axis=1,
        )
        placed[index] = jnp.dot(chosen, unit[...], preferred_element_type=F32).astype(BF16)
        for part in range(per):
            dest = index * per + part

            @pl.when(dest != trow)
            def _():
                strip_copy(index, part, dest, row).start()

            @pl.when(dest == trow)
            def _():
                land[row] = placed[index, pl.ds(part * chunk, chunk)]

    @pl.when(moved)
    def _():
        for swap in swaps[:2]:
            swap_copy(*swap).wait()

    for y in range(th):
        for x in range(nb):
            lo = (y * nb + x) * bw
            vpad[0, 1 + y, 1 + x] = begun[:, lo : lo + bw]
    halo_start(vpad.at[0], 0)

    group = max(1, 16 // sw)
    span = group * sw
    in_block = bw // span

    @pl.loop(0, rows_n // group)
    def _(step):
        first = lax.rem(row // group + step, rows_n // group)
        for i in range(group):
            source = first * group + i

            @pl.when(source != row)
            def _():
                strip_copy(0, 0, trow, source).wait_recv()

        rows = pl.ds(pl.multiple_of(lax.rem(first, in_block) * span, span), span)
        x = 1 + first // in_block
        if group == 1:
            for y in range(th):
                fpad[1 + y, x, rows, :] = land[first, y * sw : (y + 1) * sw, :]
        else:
            wide = [land[first * group + i].astype(F32) for i in range(group)]
            for y in range(th):
                joined = jnp.concatenate([w[y * sw : (y + 1) * sw] for w in wide], axis=0)
                fpad[1 + y, x, rows, :] = joined.astype(BF16)

    halo_start(fpad, ITERS, range(4))

    def tile(y, x, dy, dx):
        offset = (dy + 1) * 3 + dx + 1
        block = y * nb + x
        near = fpad[1 + y + dy, 1 + x + dx]
        own = fpad[1 + y, 1 + x]
        dots = lax.dot_general(
            near, own, (((1,), (1,)), ((), ())), preferred_element_type=F32
        )
        at_row, at_col = trow * th + y + dy, col * nb + x + dx
        inside = (at_row >= 0) & (at_row < rows_n * th)
        inside &= (at_col >= 0) & (at_col < cols_n * nb)
        link = jnp.where(inside, 1.0, 0.0).astype(F32)
        if offset != 4:
            link = link * linked[offset * blocks + block]
        value = jnp.exp(SHARPNESS * (dots - 1.0)) * link
        deg[block] += jnp.sum(value, axis=0, keepdims=True)
        high = value.astype(BF16)
        thi[block, offset * bw : (offset + 1) * bw, :] = high
        tlo[block, offset * bw : (offset + 1) * bw, :] = (value - high.astype(F32)).astype(BF16)

    def tiles(y, dy):
        @pl.loop(0, nb)
        def _(x):
            tile(y, x, dy, 0)

        @pl.loop(1, nb)
        def _(x):
            tile(y, x, dy, -1)
            tile(y, x - 1, dy, 1)

    def side_tiles(y, dy):
        tile(y, 0, dy, -1)
        tile(y, nb - 1, dy, 1)

    inner = [(y, dy) for y in range(th) for dy in (-1, 0, 1) if 0 <= y + dy < th]
    for y, dy in inner:
        tiles(y, dy)
    halo_wait(fpad, ITERS, (2, 3))
    for y, dy in inner:
        side_tiles(y, dy)
    edges = (((0, -1), 1, (6, 7)), ((th - 1, 1), 0, (4, 5)))
    for edge, way, corners in edges:
        halo_wait(fpad, ITERS, (way,))
        for corner in corners:
            corner_when(corner, lambda copy: copy.start())
        tiles(*edge)
    for edge, way, corners in edges:
        halo_wait(fpad, ITERS, corners)
        side_tiles(*edge)
    deg[...] = 1.0 / deg[...]

    def gram_copy(stage, dest, source):
        return pltpu.make_async_remote_copy(
            src_ref=gsend.at[stage],
            dst_ref=grecv.at[stage, source],
            send_sem=gram_send.at[stage, dest],
            recv_sem=gram_recv.at[stage, source],
            device_id=at(dest),
            device_id_type=pl.DeviceIdType.MESH,
        )

    pack = LANES // vec_n
    part_rows = vec_n // pack
    inverse = None
    for step in range(ITERS):
        halo_wait(vpad.at[step], step)

        @pl.loop(0, blocks)
        def _(block):
            y, x = block // nb, lax.rem(block, nb)
            field = jnp.concatenate(
                [vpad[step, y + o // 3, x + o % 3] for o in range(9)], axis=1
            )
            high = field.astype(BF16)
            low = (field - high.astype(F32)).astype(BF16)
            both = jnp.dot(
                jnp.concatenate([high, low], axis=0), thi[block], preferred_element_type=F32
            )
            total = both[:vec_n] + both[vec_n:]
            total += jnp.dot(high, tlo[block], preferred_element_type=F32)
            grown[:, pl.ds(pl.multiple_of(block * bw, bw), bw)] = total * deg[block]

        value = grown[...]
        if step:
            total = jnp.zeros((part_rows, LANES), F32)
            last = step - 1

            def add(source, total):
                @pl.when(source != me)
                def _():
                    gram_copy(last, me, source).wait_recv()

                return total + grecv[last, source]

            total = lax.fori_loop(0, peers, add, total)
            gram = jnp.concatenate(
                [total[:, i * vec_n : (i + 1) * vec_n] for i in range(pack)], axis=0
            )
            inverse = whiten(gram)
            value = jnp.dot(inverse, value, precision=HIGHEST, preferred_element_type=F32)
            grown[...] = value
        if step + 1 < ITERS:
            for y in range(th):
                for x in range(nb):
                    lo = (y * nb + x) * bw
                    vpad[step + 1, 1 + y, 1 + x] = value[:, lo : lo + bw]
            halo_start(vpad.at[step + 1], step + 1)
        gram = lax.dot_general(
            value, value, (((1,), (1,)), ((), ())),
            precision=HIGHEST, preferred_element_type=F32,
        )
        packed = jnp.concatenate(
            [gram[i * part_rows : (i + 1) * part_rows] for i in range(pack)], axis=1
        )
        gsend[step] = packed
        grecv[step, me] = packed

        @pl.loop(1, peers)
        def _(other):
            gram_copy(step, lax.rem(me + other, peers), me).start()

        if step + 1 == ITERS:
            @pl.when(moved)
            def _():
                swap_copy(*swaps[2]).start()

            @pl.when(jnp.logical_not(moved))
            def _():
                swapped[...] = value

    def add(source, total):
        @pl.when(source != me)
        def _():
            gram_copy(ITERS - 1, me, source).wait_recv()

        return total + grecv[ITERS - 1, source]

    total = lax.fori_loop(0, peers, add, jnp.zeros((part_rows, LANES), F32))
    gram = jnp.concatenate(
        [total[:, i * vec_n : (i + 1) * vec_n] for i in range(pack)], axis=0
    )
    inverse = whiten(gram)

    @pl.when(moved)
    def _():
        swap_copy(*swaps[2]).wait()

    out_ref[...] = jnp.dot(
        inverse, swapped[...], precision=HIGHEST, preferred_element_type=F32
    ) * scale

    for step in range(ITERS):
        halo_finish(vpad.at[step], step)

        @pl.loop(1, peers)
        def _(other):
            gram_copy(step, lax.rem(me + other, peers), me).wait_send()

    halo_finish(fpad, ITERS, range(4))
    for way in range(4, 8):
        corner_when(way, lambda copy: copy.wait_send())

    @pl.loop(0, rows_n)
    def _(dest):
        @pl.when(dest != trow)
        def _():
            strip_copy(0, 0, dest, row).wait_send()


def body(features, seq_order, block_links, start_vectors):
    rows_n = lax.axis_size("row")
    cols_n = lax.axis_size("col")
    tokens, width = features.shape
    vec_n, th, tile_w = start_vectors.shape
    nb = block_links.shape[2]
    sw = tile_w // rows_n
    bw = tile_w // nb
    peers = rows_n * cols_n
    blocks = th * nb
    scale = math.sqrt(th * rows_n * tile_w * cols_n)
    part_rows = vec_n * vec_n // LANES
    links = (block_links == 1).astype(F32).reshape(9 * blocks, 1, 1)
    links = jnp.broadcast_to(links, (9 * blocks, 1, LANES))
    vmem = pl.BlockSpec(memory_space=pltpu.VMEM)
    dma = pltpu.SemaphoreType.DMA
    out = pl.pallas_call(
        functools.partial(kernel, rows_n, cols_n, th, nb, sw, scale),
        out_shape=jax.ShapeDtypeStruct((vec_n, tokens), F32),
        in_specs=[vmem] * 4,
        out_specs=vmem,
        scratch_shapes=[
            pltpu.VMEM((tokens, width), BF16),
            pltpu.VMEM((tokens // LANES, LANES, width), BF16),
            pltpu.VMEM((rows_n, th * sw, width), BF16),
            pltpu.VMEM((th + 2, nb + 2, bw, width), BF16),
            pltpu.VMEM((blocks, 9 * bw, bw), BF16),
            pltpu.VMEM((blocks, 9 * bw, bw), BF16),
            pltpu.VMEM((blocks, 1, bw), F32),
            pltpu.VMEM((ITERS, th + 2, nb + 2, vec_n, bw), F32),
            pltpu.VMEM((vec_n, tokens), F32),
            pltpu.VMEM((ITERS, part_rows, LANES), F32),
            pltpu.VMEM((ITERS, peers, part_rows, LANES), F32),
            pltpu.VMEM((vec_n, tokens), F32),
            pltpu.VMEM((9 * blocks, 1, LANES), F32),
            pltpu.VMEM((vec_n, tokens), F32),
            dma((rows_n,)),
            dma((rows_n,)),
            dma((ITERS + 1, len(STEPS))),
            dma((ITERS + 1, len(STEPS))),
            dma((ITERS, peers)),
            dma((ITERS, peers)),
            dma((3,)),
            dma((3,)),
        ],
        compiler_params=pltpu.CompilerParams(
            collective_id=0, has_side_effects=True, vmem_limit_bytes=48 * 2**20
        ),
    )(features, seq_order, links, start_vectors.reshape(vec_n, tokens))
    return out.reshape(vec_n, th, tile_w)


def solution(mesh):
    return jax.shard_map(
        body,
        mesh=mesh,
        in_specs=(
            P(("slide", "row", "col"), None),
            P(("slide", "row", "col"), None),
            P(None, ("slide", "row"), "col"),
            P(None, ("slide", "row"), "col"),
        ),
        out_specs=P(None, ("slide", "row"), "col"),
        check_vma=False,
    )
```

```python
import functools
import math

import jax
import jax.numpy as jnp
from jax import lax
from jax.experimental import pallas as pl
from jax.experimental.pallas import tpu as pltpu
from jax.sharding import PartitionSpec as P

ITERS = 3
SHARPNESS = 4.0
EPSILON = 1e-06
HIGHEST = lax.Precision.HIGHEST
F32 = jnp.float32
BF16 = jnp.bfloat16
LANES = 128
STEPS = ((-1, 0), (1, 0), (0, -1), (0, 1), (-1, -1), (-1, 1), (1, -1), (1, 1))


def snake(place, rows_n):
    if rows_n % 4:
        return place
    odd_pair = lax.rem(place // 2, 2)
    return place + odd_pair * (1 - 2 * lax.rem(place, 2))


def whiten(gram):
    k = gram.shape[0]
    rows = lax.broadcasted_iota(jnp.int32, (k, k), 0)
    cols = lax.broadcasted_iota(jnp.int32, (k, k), 1)
    eye = (rows == cols).astype(F32)
    work = jnp.concatenate([gram, eye], axis=1)
    at = lax.broadcasted_iota(jnp.int32, (k, 1), 0)
    for step in range(k - 1):
        pivot = work[step : step + 1, :]
        pivot = pivot / pivot[:, step : step + 1]
        below = jnp.where(at > step, work[:, step : step + 1], 0.0)
        work = work - below * pivot
    diag = jnp.sum(work[:, :k] * eye, axis=1, keepdims=True)
    return work[:, k:] / jnp.sqrt(diag)


def kernel(
    rows_n, cols_n, th, nb, sw, scale,
    feat_ref, seq_ref, link_ref, start_ref, out_ref,
    unit, placed, land, fpad, thi, tlo, deg, vpad, grown, gsend, grecv,
    begun, linked, swapped,
    a2a_send, a2a_recv, halo_send, halo_recv, gram_send, gram_recv, swap_send, swap_recv,
    row_send, row_recv,
):
    row, col = lax.axis_index("row"), lax.axis_index("col")
    peers = rows_n * cols_n
    me = row * cols_n + col
    trow = snake(row, rows_n)
    moved = trow != row
    tokens, width = feat_ref.shape
    vec_n = start_ref.shape[0]
    bw = LANES
    blocks = th * nb
    chunk = th * sw
    per = LANES // chunk
    supers = tokens // LANES

    def at(peer):
        return {"row": peer // cols_n, "col": lax.rem(peer, cols_n)}

    def exists(dr, dc):
        r, c = trow + dr, col + dc
        return (r >= 0) & (r < rows_n) & (c >= 0) & (c < cols_n)

    def piece(buf, dr, dc, arriving):
        def pick(step, n):
            if step == 0:
                return pl.ds(1, n)
            if arriving:
                return pl.ds(n + 1 if step < 0 else 0, 1)
            return pl.ds(1 if step < 0 else n, 1)

        return buf.at[pick(dr, th), pick(dc, nb)]

    def halo_copy(buf, stage, way, sending):
        dr, dc = STEPS[way]
        r = snake(trow + dr if sending else trow - dr, rows_n)
        c = col + dc if sending else col - dc
        return pltpu.make_async_remote_copy(
            src_ref=piece(buf, dr, dc, False),
            dst_ref=piece(buf, dr, dc, True),
            send_sem=halo_send.at[stage, way],
            recv_sem=halo_recv.at[stage, way],
            device_id={"row": r, "col": c},
            device_id_type=pl.DeviceIdType.MESH,
        )

    def halo_start(buf, stage, ways=range(8)):
        for way in ways:
            dr, dc = STEPS[way]

            @pl.when(exists(dr, dc))
            def _():
                halo_copy(buf, stage, way, True).start()

    def halo_wait(buf, stage, ways=range(8)):
        for way in ways:
            dr, dc = STEPS[way]

            @pl.when(exists(-dr, -dc))
            def _():
                halo_copy(buf, stage, way, False).wait_recv()

    def halo_finish(buf, stage, ways=range(8)):
        for way in ways:
            dr, dc = STEPS[way]

            @pl.when(exists(dr, dc))
            def _():
                halo_copy(buf, stage, way, True).wait_send()

    def row_copy(way, x, sending):
        dr = STEPS[way][0]
        return pltpu.make_async_remote_copy(
            src_ref=fpad.at[1 if dr < 0 else th, 1 + x],
            dst_ref=fpad.at[th + 1 if dr < 0 else 0, 1 + x],
            send_sem=row_send.at[way, x],
            recv_sem=row_recv.at[way, x],
            device_id={"row": snake(trow + dr if sending else trow - dr, rows_n)},
            device_id_type=pl.DeviceIdType.MESH,
        )

    def corner_copy(way):
        dr, dc = STEPS[way]
        edge = pl.ds(th + 1 if dr < 0 else 0, 1)
        return pltpu.make_async_remote_copy(
            src_ref=fpad.at[edge, pl.ds(1 if dc < 0 else nb, 1)],
            dst_ref=fpad.at[edge, pl.ds(nb + 1 if dc < 0 else 0, 1)],
            send_sem=halo_send.at[ITERS, way],
            recv_sem=halo_recv.at[ITERS, way],
            device_id={"col": col + dc},
            device_id_type=pl.DeviceIdType.MESH,
        )

    def corner_when(way, action, ready=True):
        dr, dc = STEPS[way]

        @pl.when(exists(-dr, dc) & ready)
        def _():
            action(corner_copy(way))

    def swap_copy(src, dst, index):
        return pltpu.make_async_remote_copy(
            src_ref=src,
            dst_ref=dst,
            send_sem=swap_send.at[index],
            recv_sem=swap_recv.at[index],
            device_id={"row": trow},
            device_id_type=pl.DeviceIdType.MESH,
        )

    swaps = (
        (start_ref, begun, 0),
        (link_ref, linked, 1),
        (grown, swapped, 2),
    )

    def halo_zero(buf):
        for dr, dc in STEPS:
            @pl.when(jnp.logical_not(exists(-dr, -dc)))
            def _():
                where = piece(buf, dr, dc, True)
                where[...] = jnp.zeros(where.shape, where.dtype)

    barrier = pltpu.get_barrier_semaphore()

    @pl.loop(1, peers)
    def _(step):
        pl.semaphore_signal(
            barrier, inc=1, device_id=at(lax.rem(me + step, peers)),
            device_id_type=pl.DeviceIdType.MESH,
        )

    for step in range(ITERS):
        halo_zero(vpad.at[step])
    halo_zero(fpad)
    deg[...] = jnp.zeros_like(deg)

    @pl.loop(0, tokens // 64)
    def _(step):
        rows = pl.ds(pl.multiple_of(step * 64, 64), 64)
        wide = feat_ref[rows, :].astype(F32)
        squares = jnp.sum(wide * wide, axis=1, keepdims=True)
        unit[rows, :] = (wide * lax.rsqrt(squares + EPSILON)).astype(BF16)

    pl.semaphore_wait(barrier, peers - 1)

    @pl.when(moved)
    def _():
        for swap in swaps[:2]:
            swap_copy(*swap).start()

    @pl.when(jnp.logical_not(moved))
    def _():
        begun[...] = start_ref[...]
        linked[...] = link_ref[...]

    def strip_copy(index, part, dest, source):
        return pltpu.make_async_remote_copy(
            src_ref=placed.at[index, pl.ds(part * chunk, chunk)],
            dst_ref=land.at[source],
            send_sem=a2a_send.at[dest],
            recv_sem=a2a_recv.at[source],
            device_id={"row": snake(dest, rows_n)},
            device_id_type=pl.DeviceIdType.MESH,
        )

    @pl.loop(0, supers)
    def _(step):
        index = lax.rem(trow // per + 1 + step, supers)
        order = seq_ref[:, pl.ds(pl.multiple_of(index * LANES, LANES), LANES)]
        order = jnp.broadcast_to(order.astype(F32), (LANES, LANES)).T
        lane = lax.broadcasted_iota(jnp.int32, (LANES, LANES), 1).astype(F32)
        chosen = jnp.concatenate(
            [
                jnp.where(order == lane + float(j * LANES), 1.0, 0.0).astype(BF16)
                for j in range(supers)
            ],
            axis=1,
        )
        placed[index] = jnp.dot(chosen, unit[...], preferred_element_type=F32).astype(BF16)
        for part in range(per):
            dest = index * per + part

            @pl.when(dest != trow)
            def _():
                strip_copy(index, part, dest, row).start()

            @pl.when(dest == trow)
            def _():
                land[row] = placed[index, pl.ds(part * chunk, chunk)]

    @pl.when(moved)
    def _():
        for swap in swaps[:2]:
            swap_copy(*swap).wait()

    for y in range(th):
        for x in range(nb):
            lo = (y * nb + x) * bw
            vpad[0, 1 + y, 1 + x] = begun[:, lo : lo + bw]
    halo_start(vpad.at[0], 0)

    group = max(1, 16 // sw)
    span = group * sw
    strips = bw // sw

    def block_at(step):
        return lax.rem(row // strips + step, nb)

    @pl.loop(0, nb)
    def _(step):
        x = block_at(step)
        for i in range(strips // group):
            first = x * strips + i * group
            for j in range(group):
                source = first + j

                @pl.when(source != row)
                def _():
                    strip_copy(0, 0, trow, source).wait_recv()

            rows = slice(i * span, (i + 1) * span)
            if group == 1:
                for y in range(th):
                    fpad[1 + y, 1 + x, rows, :] = land[first, y * sw : (y + 1) * sw, :]
            else:
                wide = [land[first + j].astype(F32) for j in range(group)]
                for y in range(th):
                    joined = jnp.concatenate([w[y * sw : (y + 1) * sw] for w in wide], axis=0)
                    fpad[1 + y, 1 + x, rows, :] = joined.astype(BF16)
        for way in (0, 1):
            @pl.when(exists(STEPS[way][0], 0))
            def _():
                row_copy(way, x, True).start()

    halo_start(fpad, ITERS, (2, 3))

    def tile(y, x, dy, dx):
        offset = (dy + 1) * 3 + dx + 1
        block = y * nb + x
        near = fpad[1 + y + dy, 1 + x + dx]
        own = fpad[1 + y, 1 + x]
        dots = lax.dot_general(
            near, own, (((1,), (1,)), ((), ())), preferred_element_type=F32
        )
        at_row, at_col = trow * th + y + dy, col * nb + x + dx
        inside = (at_row >= 0) & (at_row < rows_n * th)
        inside &= (at_col >= 0) & (at_col < cols_n * nb)
        link = jnp.where(inside, 1.0, 0.0).astype(F32)
        if offset != 4:
            link = link * linked[offset * blocks + block]
        value = jnp.exp(SHARPNESS * (dots - 1.0)) * link
        deg[block] += jnp.sum(value, axis=0, keepdims=True)
        high = value.astype(BF16)
        thi[block, offset * bw : (offset + 1) * bw, :] = high
        tlo[block, offset * bw : (offset + 1) * bw, :] = (value - high.astype(F32)).astype(BF16)

    def tiles(y, dy):
        @pl.loop(0, nb)
        def _(x):
            tile(y, x, dy, 0)

        @pl.loop(1, nb)
        def _(x):
            tile(y, x, dy, -1)
            tile(y, x - 1, dy, 1)

    def side_tiles(y, dy):
        tile(y, 0, dy, -1)
        tile(y, nb - 1, dy, 1)

    inner = [(y, dy) for y in range(th) for dy in (-1, 0, 1) if 0 <= y + dy < th]
    for y, dy in inner:
        tiles(y, dy)
    halo_wait(fpad, ITERS, (2, 3))
    for y, dy in inner:
        side_tiles(y, dy)
    edges = (((0, -1), 1, (6, 7)), ((th - 1, 1), 0, (4, 5)))

    @pl.loop(0, nb)
    def _(step):
        x = block_at(step)
        for (y, dy), way, corners in edges:
            @pl.when(exists(-STEPS[way][0], 0))
            def _():
                row_copy(way, x, False).wait_recv()

            for corner in corners:
                last = 0 if STEPS[corner][1] < 0 else nb - 1
                corner_when(corner, lambda copy: copy.start(), x == last)
            tile(y, x, dy, 0)

            @pl.when(x > 0)
            def _():
                tile(y, x - 1, dy, 1)

            @pl.when(x < nb - 1)
            def _():
                tile(y, x + 1, dy, -1)

    for edge, way, corners in edges:
        halo_wait(fpad, ITERS, corners)
        side_tiles(*edge)
    deg[...] = 1.0 / deg[...]

    def gram_copy(stage, dest, source):
        return pltpu.make_async_remote_copy(
            src_ref=gsend.at[stage],
            dst_ref=grecv.at[stage, source],
            send_sem=gram_send.at[stage, dest],
            recv_sem=gram_recv.at[stage, source],
            device_id=at(dest),
            device_id_type=pl.DeviceIdType.MESH,
        )

    pack = LANES // vec_n
    part_rows = vec_n // pack
    inverse = None
    for step in range(ITERS):
        halo_wait(vpad.at[step], step)

        @pl.loop(0, blocks)
        def _(block):
            y, x = block // nb, lax.rem(block, nb)
            field = jnp.concatenate(
                [vpad[step, y + o // 3, x + o % 3] for o in range(9)], axis=1
            )
            high = field.astype(BF16)
            low = (field - high.astype(F32)).astype(BF16)
            both = jnp.dot(
                jnp.concatenate([high, low], axis=0), thi[block], preferred_element_type=F32
            )
            total = both[:vec_n] + both[vec_n:]
            total += jnp.dot(high, tlo[block], preferred_element_type=F32)
            grown[:, pl.ds(pl.multiple_of(block * bw, bw), bw)] = total * deg[block]

        value = grown[...]
        if step:
            total = jnp.zeros((part_rows, LANES), F32)
            last = step - 1

            def add(source, total):
                @pl.when(source != me)
                def _():
                    gram_copy(last, me, source).wait_recv()

                return total + grecv[last, source]

            total = lax.fori_loop(0, peers, add, total)
            gram = jnp.concatenate(
                [total[:, i * vec_n : (i + 1) * vec_n] for i in range(pack)], axis=0
            )
            inverse = whiten(gram)
            value = jnp.dot(inverse, value, precision=HIGHEST, preferred_element_type=F32)
            grown[...] = value
        if step + 1 < ITERS:
            for y in range(th):
                for x in range(nb):
                    lo = (y * nb + x) * bw
                    vpad[step + 1, 1 + y, 1 + x] = value[:, lo : lo + bw]
            halo_start(vpad.at[step + 1], step + 1)
        gram = lax.dot_general(
            value, value, (((1,), (1,)), ((), ())),
            precision=HIGHEST, preferred_element_type=F32,
        )
        packed = jnp.concatenate(
            [gram[i * part_rows : (i + 1) * part_rows] for i in range(pack)], axis=1
        )
        gsend[step] = packed
        grecv[step, me] = packed

        @pl.loop(1, peers)
        def _(other):
            gram_copy(step, lax.rem(me + other, peers), me).start()

        if step + 1 == ITERS:
            @pl.when(moved)
            def _():
                swap_copy(*swaps[2]).start()

            @pl.when(jnp.logical_not(moved))
            def _():
                swapped[...] = value

    def add(source, total):
        @pl.when(source != me)
        def _():
            gram_copy(ITERS - 1, me, source).wait_recv()

        return total + grecv[ITERS - 1, source]

    total = lax.fori_loop(0, peers, add, jnp.zeros((part_rows, LANES), F32))
    gram = jnp.concatenate(
        [total[:, i * vec_n : (i + 1) * vec_n] for i in range(pack)], axis=0
    )
    inverse = whiten(gram)

    @pl.when(moved)
    def _():
        swap_copy(*swaps[2]).wait()

    out_ref[...] = jnp.dot(
        inverse, swapped[...], precision=HIGHEST, preferred_element_type=F32
    ) * scale

    for step in range(ITERS):
        halo_finish(vpad.at[step], step)

        @pl.loop(1, peers)
        def _(other):
            gram_copy(step, lax.rem(me + other, peers), me).wait_send()

    halo_finish(fpad, ITERS, (2, 3))

    @pl.loop(0, nb)
    def _(x):
        for way in (0, 1):
            @pl.when(exists(STEPS[way][0], 0))
            def _():
                row_copy(way, x, True).wait_send()

    for way in range(4, 8):
        corner_when(way, lambda copy: copy.wait_send())

    @pl.loop(0, rows_n)
    def _(dest):
        @pl.when(dest != trow)
        def _():
            strip_copy(0, 0, dest, row).wait_send()


def body(features, seq_order, block_links, start_vectors):
    rows_n = lax.axis_size("row")
    cols_n = lax.axis_size("col")
    tokens, width = features.shape
    vec_n, th, tile_w = start_vectors.shape
    nb = block_links.shape[2]
    sw = tile_w // rows_n
    bw = tile_w // nb
    peers = rows_n * cols_n
    blocks = th * nb
    scale = math.sqrt(th * rows_n * tile_w * cols_n)
    part_rows = vec_n * vec_n // LANES
    links = (block_links == 1).astype(F32).reshape(9 * blocks, 1, 1)
    links = jnp.broadcast_to(links, (9 * blocks, 1, LANES))
    vmem = pl.BlockSpec(memory_space=pltpu.VMEM)
    dma = pltpu.SemaphoreType.DMA
    out = pl.pallas_call(
        functools.partial(kernel, rows_n, cols_n, th, nb, sw, scale),
        out_shape=jax.ShapeDtypeStruct((vec_n, tokens), F32),
        in_specs=[vmem] * 4,
        out_specs=vmem,
        scratch_shapes=[
            pltpu.VMEM((tokens, width), BF16),
            pltpu.VMEM((tokens // LANES, LANES, width), BF16),
            pltpu.VMEM((rows_n, th * sw, width), BF16),
            pltpu.VMEM((th + 2, nb + 2, bw, width), BF16),
            pltpu.VMEM((blocks, 9 * bw, bw), BF16),
            pltpu.VMEM((blocks, 9 * bw, bw), BF16),
            pltpu.VMEM((blocks, 1, bw), F32),
            pltpu.VMEM((ITERS, th + 2, nb + 2, vec_n, bw), F32),
            pltpu.VMEM((vec_n, tokens), F32),
            pltpu.VMEM((ITERS, part_rows, LANES), F32),
            pltpu.VMEM((ITERS, peers, part_rows, LANES), F32),
            pltpu.VMEM((vec_n, tokens), F32),
            pltpu.VMEM((9 * blocks, 1, LANES), F32),
            pltpu.VMEM((vec_n, tokens), F32),
            dma((rows_n,)),
            dma((rows_n,)),
            dma((ITERS + 1, len(STEPS))),
            dma((ITERS + 1, len(STEPS))),
            dma((ITERS, peers)),
            dma((ITERS, peers)),
            dma((3,)),
            dma((3,)),
            dma((2, nb)),
            dma((2, nb)),
        ],
        compiler_params=pltpu.CompilerParams(
            collective_id=0, has_side_effects=True, vmem_limit_bytes=48 * 2**20
        ),
    )(features, seq_order, links, start_vectors.reshape(vec_n, tokens))
    return out.reshape(vec_n, th, tile_w)


def solution(mesh):
    return jax.shard_map(
        body,
        mesh=mesh,
        in_specs=(
            P(("slide", "row", "col"), None),
            P(("slide", "row", "col"), None),
            P(None, ("slide", "row"), "col"),
            P(None, ("slide", "row"), "col"),
        ),
        out_specs=P(None, ("slide", "row"), "col"),
        check_vma=False,
    )
```

```python
import functools
import math

import jax
import jax.numpy as jnp
from jax import lax
from jax.experimental import pallas as pl
from jax.experimental.pallas import tpu as pltpu
from jax.sharding import PartitionSpec as P

ITERS = 3
SHARPNESS = 4.0
EPSILON = 1e-06
HIGHEST = lax.Precision.HIGHEST
F32 = jnp.float32
BF16 = jnp.bfloat16
LANES = 128
STEPS = ((-1, 0), (1, 0), (0, -1), (0, 1), (-1, -1), (-1, 1), (1, -1), (1, 1))


def snake(place, rows_n):
    if rows_n % 4:
        return place
    odd_pair = lax.rem(place // 2, 2)
    return place + odd_pair * (1 - 2 * lax.rem(place, 2))


def whiten(gram):
    k = gram.shape[0]
    rows = lax.broadcasted_iota(jnp.int32, (k, k), 0)
    cols = lax.broadcasted_iota(jnp.int32, (k, k), 1)
    eye = (rows == cols).astype(F32)
    work = jnp.concatenate([gram, eye], axis=1)
    at = lax.broadcasted_iota(jnp.int32, (k, 1), 0)
    for step in range(k - 1):
        pivot = work[step : step + 1, :]
        pivot = pivot / pivot[:, step : step + 1]
        below = jnp.where(at > step, work[:, step : step + 1], 0.0)
        work = work - below * pivot
    diag = jnp.sum(work[:, :k] * eye, axis=1, keepdims=True)
    return work[:, k:] / jnp.sqrt(diag)


def kernel(
    rows_n, cols_n, th, nb, sw, scale,
    feat_ref, seq_ref, link_ref, start_ref, out_ref,
    unit, placed, land, fpad, thi, tlo, deg, vpad, grown, gsend, grecv,
    begun, linked, swapped,
    a2a_send, a2a_recv, halo_send, halo_recv, gram_send, gram_recv, swap_send, swap_recv,
    solved,
):
    row, col = lax.axis_index("row"), lax.axis_index("col")
    peers = rows_n * cols_n
    me = row * cols_n + col
    trow = snake(row, rows_n)
    moved = trow != row
    tokens, width = feat_ref.shape
    vec_n = start_ref.shape[0]
    bw = LANES
    blocks = th * nb
    chunk = th * sw
    per = LANES // chunk
    supers = tokens // LANES

    def at(peer):
        return {"row": peer // cols_n, "col": lax.rem(peer, cols_n)}

    def exists(dr, dc):
        r, c = trow + dr, col + dc
        return (r >= 0) & (r < rows_n) & (c >= 0) & (c < cols_n)

    def piece(buf, dr, dc, arriving):
        def pick(step, n):
            if step == 0:
                return pl.ds(1, n)
            if arriving:
                return pl.ds(n + 1 if step < 0 else 0, 1)
            return pl.ds(1 if step < 0 else n, 1)

        return buf.at[pick(dr, th), pick(dc, nb)]

    def halo_copy(buf, stage, way, sending):
        dr, dc = STEPS[way]
        r = snake(trow + dr if sending else trow - dr, rows_n)
        c = col + dc if sending else col - dc
        return pltpu.make_async_remote_copy(
            src_ref=piece(buf, dr, dc, False),
            dst_ref=piece(buf, dr, dc, True),
            send_sem=halo_send.at[stage, way],
            recv_sem=halo_recv.at[stage, way],
            device_id={"row": r, "col": c},
            device_id_type=pl.DeviceIdType.MESH,
        )

    def halo_start(buf, stage, ways=range(8)):
        for way in ways:
            dr, dc = STEPS[way]

            @pl.when(exists(dr, dc))
            def _():
                halo_copy(buf, stage, way, True).start()

    def halo_wait(buf, stage, ways=range(8)):
        for way in ways:
            dr, dc = STEPS[way]

            @pl.when(exists(-dr, -dc))
            def _():
                halo_copy(buf, stage, way, False).wait_recv()

    def halo_finish(buf, stage, ways=range(8)):
        for way in ways:
            dr, dc = STEPS[way]

            @pl.when(exists(dr, dc))
            def _():
                halo_copy(buf, stage, way, True).wait_send()

    def corner_copy(way):
        dr, dc = STEPS[way]
        edge = pl.ds(th + 1 if dr < 0 else 0, 1)
        return pltpu.make_async_remote_copy(
            src_ref=fpad.at[edge, pl.ds(1 if dc < 0 else nb, 1)],
            dst_ref=fpad.at[edge, pl.ds(nb + 1 if dc < 0 else 0, 1)],
            send_sem=halo_send.at[ITERS, way],
            recv_sem=halo_recv.at[ITERS, way],
            device_id={"col": col + dc},
            device_id_type=pl.DeviceIdType.MESH,
        )

    def corner_when(way, action):
        dr, dc = STEPS[way]

        @pl.when(exists(-dr, dc))
        def _():
            action(corner_copy(way))

    def swap_copy(src, dst, index):
        return pltpu.make_async_remote_copy(
            src_ref=src,
            dst_ref=dst,
            send_sem=swap_send.at[index],
            recv_sem=swap_recv.at[index],
            device_id={"row": trow},
            device_id_type=pl.DeviceIdType.MESH,
        )

    swaps = (
        (start_ref, begun, 0),
        (link_ref, linked, 1),
        (grown, swapped, 2),
    )

    def halo_zero(buf):
        for dr, dc in STEPS:
            @pl.when(jnp.logical_not(exists(-dr, -dc)))
            def _():
                where = piece(buf, dr, dc, True)
                where[...] = jnp.zeros(where.shape, where.dtype)

    barrier = pltpu.get_barrier_semaphore()

    @pl.loop(1, peers)
    def _(step):
        pl.semaphore_signal(
            barrier, inc=1, device_id=at(lax.rem(me + step, peers)),
            device_id_type=pl.DeviceIdType.MESH,
        )

    for step in range(ITERS):
        halo_zero(vpad.at[step])
    halo_zero(fpad)
    deg[...] = jnp.zeros_like(deg)

    @pl.loop(0, tokens // 64)
    def _(step):
        rows = pl.ds(pl.multiple_of(step * 64, 64), 64)
        wide = feat_ref[rows, :].astype(F32)
        squares = jnp.sum(wide * wide, axis=1, keepdims=True)
        unit[rows, :] = (wide * lax.rsqrt(squares + EPSILON)).astype(BF16)

    pl.semaphore_wait(barrier, peers - 1)

    @pl.when(moved)
    def _():
        for swap in swaps[:2]:
            swap_copy(*swap).start()

    @pl.when(jnp.logical_not(moved))
    def _():
        begun[...] = start_ref[...]
        linked[...] = link_ref[...]

    def strip_copy(index, part, dest, source):
        return pltpu.make_async_remote_copy(
            src_ref=placed.at[index, pl.ds(part * chunk, chunk)],
            dst_ref=land.at[source],
            send_sem=a2a_send.at[dest],
            recv_sem=a2a_recv.at[source],
            device_id={"row": snake(dest, rows_n)},
            device_id_type=pl.DeviceIdType.MESH,
        )

    @pl.loop(0, supers)
    def _(step):
        index = lax.rem(trow // per + 1 + step, supers)
        order = seq_ref[:, pl.ds(pl.multiple_of(index * LANES, LANES), LANES)]
        order = jnp.broadcast_to(order.astype(F32), (LANES, LANES)).T
        lane = lax.broadcasted_iota(jnp.int32, (LANES, LANES), 1).astype(F32)
        chosen = jnp.concatenate(
            [
                jnp.where(order == lane + float(j * LANES), 1.0, 0.0).astype(BF16)
                for j in range(supers)
            ],
            axis=1,
        )
        placed[index] = jnp.dot(chosen, unit[...], preferred_element_type=F32).astype(BF16)
        for part in range(per):
            dest = index * per + part

            @pl.when(dest != trow)
            def _():
                strip_copy(index, part, dest, row).start()

            @pl.when(dest == trow)
            def _():
                land[row] = placed[index, pl.ds(part * chunk, chunk)]

    @pl.when(moved)
    def _():
        for swap in swaps[:2]:
            swap_copy(*swap).wait()

    for y in range(th):
        for x in range(nb):
            lo = (y * nb + x) * bw
            vpad[0, 1 + y, 1 + x] = begun[:, lo : lo + bw]
    halo_start(vpad.at[0], 0)

    group = max(1, 16 // sw)
    span = group * sw
    in_block = bw // span

    @pl.loop(0, rows_n // group)
    def _(step):
        first = lax.rem(row // group + step, rows_n // group)
        for i in range(group):
            source = first * group + i

            @pl.when(source != row)
            def _():
                strip_copy(0, 0, trow, source).wait_recv()

        rows = pl.ds(pl.multiple_of(lax.rem(first, in_block) * span, span), span)
        x = 1 + first // in_block
        if group == 1:
            for y in range(th):
                fpad[1 + y, x, rows, :] = land[first, y * sw : (y + 1) * sw, :]
        else:
            wide = [land[first * group + i].astype(F32) for i in range(group)]
            for y in range(th):
                joined = jnp.concatenate([w[y * sw : (y + 1) * sw] for w in wide], axis=0)
                fpad[1 + y, x, rows, :] = joined.astype(BF16)

    halo_start(fpad, ITERS, range(4))

    def tile(y, x, dy, dx):
        offset = (dy + 1) * 3 + dx + 1
        block = y * nb + x
        near = fpad[1 + y + dy, 1 + x + dx]
        own = fpad[1 + y, 1 + x]
        dots = lax.dot_general(
            near, own, (((1,), (1,)), ((), ())), preferred_element_type=F32
        )
        at_row, at_col = trow * th + y + dy, col * nb + x + dx
        inside = (at_row >= 0) & (at_row < rows_n * th)
        inside &= (at_col >= 0) & (at_col < cols_n * nb)
        link = jnp.where(inside, 1.0, 0.0).astype(F32)
        if offset != 4:
            link = link * linked[offset * blocks + block]
        value = jnp.exp(SHARPNESS * (dots - 1.0)) * link
        deg[block] += jnp.sum(value, axis=0, keepdims=True)
        high = value.astype(BF16)
        thi[block, offset * bw : (offset + 1) * bw, :] = high
        tlo[block, offset * bw : (offset + 1) * bw, :] = (value - high.astype(F32)).astype(BF16)

    def tiles(y, dy):
        @pl.loop(0, nb)
        def _(x):
            tile(y, x, dy, 0)

        @pl.loop(1, nb)
        def _(x):
            tile(y, x, dy, -1)
            tile(y, x - 1, dy, 1)

    def side_tiles(y, dy):
        tile(y, 0, dy, -1)
        tile(y, nb - 1, dy, 1)

    inner = [(y, dy) for y in range(th) for dy in (-1, 0, 1) if 0 <= y + dy < th]
    for y, dy in inner:
        tiles(y, dy)
    halo_wait(fpad, ITERS, (2, 3))
    for y, dy in inner:
        side_tiles(y, dy)
    edges = (((0, -1), 1, (6, 7)), ((th - 1, 1), 0, (4, 5)))
    for edge, way, corners in edges:
        halo_wait(fpad, ITERS, (way,))
        for corner in corners:
            corner_when(corner, lambda copy: copy.start())
        tiles(*edge)
    for edge, way, corners in edges:
        halo_wait(fpad, ITERS, corners)
        side_tiles(*edge)
    deg[...] = 1.0 / deg[...]

    def gram_copy(stage, dest, source):
        return pltpu.make_async_remote_copy(
            src_ref=gsend.at[stage],
            dst_ref=grecv.at[stage, source],
            send_sem=gram_send.at[stage, dest],
            recv_sem=gram_recv.at[stage, source],
            device_id=at(dest),
            device_id_type=pl.DeviceIdType.MESH,
        )

    pack = LANES // vec_n
    part_rows = vec_n // pack
    inverse = None
    for step in range(ITERS):
        halo_wait(vpad.at[step], step)
        if step > 1:
            before = inverse

            @pl.loop(0, (th + 2) * (nb + 2))
            def _(block):
                y, x = block // (nb + 2), lax.rem(block, nb + 2)
                solved[y, x] = jnp.dot(
                    before, vpad[step, y, x], precision=HIGHEST, preferred_element_type=F32
                )

        source_of = solved if step > 1 else vpad.at[step]

        @pl.loop(0, blocks)
        def _(block):
            y, x = block // nb, lax.rem(block, nb)
            field = jnp.concatenate(
                [source_of[y + o // 3, x + o % 3] for o in range(9)], axis=1
            )
            high = field.astype(BF16)
            low = (field - high.astype(F32)).astype(BF16)
            both = jnp.dot(
                jnp.concatenate([high, low], axis=0), thi[block], preferred_element_type=F32
            )
            total = both[:vec_n] + both[vec_n:]
            total += jnp.dot(high, tlo[block], preferred_element_type=F32)
            grown[:, pl.ds(pl.multiple_of(block * bw, bw), bw)] = total * deg[block]

        value = grown[...]
        if step + 1 < ITERS:
            for y in range(th):
                for x in range(nb):
                    lo = (y * nb + x) * bw
                    vpad[step + 1, 1 + y, 1 + x] = value[:, lo : lo + bw]
            halo_start(vpad.at[step + 1], step + 1)
        if step:
            total = jnp.zeros((part_rows, LANES), F32)
            last = step - 1

            def add(source, total):
                @pl.when(source != me)
                def _():
                    gram_copy(last, me, source).wait_recv()

                return total + grecv[last, source]

            total = lax.fori_loop(0, peers, add, total)
            gram = jnp.concatenate(
                [total[:, i * vec_n : (i + 1) * vec_n] for i in range(pack)], axis=0
            )
            inverse = whiten(gram)
            value = jnp.dot(inverse, value, precision=HIGHEST, preferred_element_type=F32)
            grown[...] = value
        gram = lax.dot_general(
            value, value, (((1,), (1,)), ((), ())),
            precision=HIGHEST, preferred_element_type=F32,
        )
        packed = jnp.concatenate(
            [gram[i * part_rows : (i + 1) * part_rows] for i in range(pack)], axis=1
        )
        gsend[step] = packed
        grecv[step, me] = packed

        @pl.loop(1, peers)
        def _(other):
            gram_copy(step, lax.rem(me + other, peers), me).start()

        if step + 1 == ITERS:
            @pl.when(moved)
            def _():
                swap_copy(*swaps[2]).start()

            @pl.when(jnp.logical_not(moved))
            def _():
                swapped[...] = value

    def add(source, total):
        @pl.when(source != me)
        def _():
            gram_copy(ITERS - 1, me, source).wait_recv()

        return total + grecv[ITERS - 1, source]

    total = lax.fori_loop(0, peers, add, jnp.zeros((part_rows, LANES), F32))
    gram = jnp.concatenate(
        [total[:, i * vec_n : (i + 1) * vec_n] for i in range(pack)], axis=0
    )
    inverse = whiten(gram)

    @pl.when(moved)
    def _():
        swap_copy(*swaps[2]).wait()

    out_ref[...] = jnp.dot(
        inverse, swapped[...], precision=HIGHEST, preferred_element_type=F32
    ) * scale

    for step in range(ITERS):
        halo_finish(vpad.at[step], step)

        @pl.loop(1, peers)
        def _(other):
            gram_copy(step, lax.rem(me + other, peers), me).wait_send()

    halo_finish(fpad, ITERS, range(4))
    for way in range(4, 8):
        corner_when(way, lambda copy: copy.wait_send())

    @pl.loop(0, rows_n)
    def _(dest):
        @pl.when(dest != trow)
        def _():
            strip_copy(0, 0, dest, row).wait_send()


def body(features, seq_order, block_links, start_vectors):
    rows_n = lax.axis_size("row")
    cols_n = lax.axis_size("col")
    tokens, width = features.shape
    vec_n, th, tile_w = start_vectors.shape
    nb = block_links.shape[2]
    sw = tile_w // rows_n
    bw = tile_w // nb
    peers = rows_n * cols_n
    blocks = th * nb
    scale = math.sqrt(th * rows_n * tile_w * cols_n)
    part_rows = vec_n * vec_n // LANES
    links = (block_links == 1).astype(F32).reshape(9 * blocks, 1, 1)
    links = jnp.broadcast_to(links, (9 * blocks, 1, LANES))
    vmem = pl.BlockSpec(memory_space=pltpu.VMEM)
    dma = pltpu.SemaphoreType.DMA
    out = pl.pallas_call(
        functools.partial(kernel, rows_n, cols_n, th, nb, sw, scale),
        out_shape=jax.ShapeDtypeStruct((vec_n, tokens), F32),
        in_specs=[vmem] * 4,
        out_specs=vmem,
        scratch_shapes=[
            pltpu.VMEM((tokens, width), BF16),
            pltpu.VMEM((tokens // LANES, LANES, width), BF16),
            pltpu.VMEM((rows_n, th * sw, width), BF16),
            pltpu.VMEM((th + 2, nb + 2, bw, width), BF16),
            pltpu.VMEM((blocks, 9 * bw, bw), BF16),
            pltpu.VMEM((blocks, 9 * bw, bw), BF16),
            pltpu.VMEM((blocks, 1, bw), F32),
            pltpu.VMEM((ITERS, th + 2, nb + 2, vec_n, bw), F32),
            pltpu.VMEM((vec_n, tokens), F32),
            pltpu.VMEM((ITERS, part_rows, LANES), F32),
            pltpu.VMEM((ITERS, peers, part_rows, LANES), F32),
            pltpu.VMEM((vec_n, tokens), F32),
            pltpu.VMEM((9 * blocks, 1, LANES), F32),
            pltpu.VMEM((vec_n, tokens), F32),
            dma((rows_n,)),
            dma((rows_n,)),
            dma((ITERS + 1, len(STEPS))),
            dma((ITERS + 1, len(STEPS))),
            dma((ITERS, peers)),
            dma((ITERS, peers)),
            dma((3,)),
            dma((3,)),
            pltpu.VMEM((th + 2, nb + 2, vec_n, bw), F32),
        ],
        compiler_params=pltpu.CompilerParams(
            collective_id=0, has_side_effects=True, vmem_limit_bytes=48 * 2**20
        ),
    )(features, seq_order, links, start_vectors.reshape(vec_n, tokens))
    return out.reshape(vec_n, th, tile_w)


def solution(mesh):
    return jax.shard_map(
        body,
        mesh=mesh,
        in_specs=(
            P(("slide", "row", "col"), None),
            P(("slide", "row", "col"), None),
            P(None, ("slide", "row"), "col"),
            P(None, ("slide", "row"), "col"),
        ),
        out_specs=P(None, ("slide", "row"), "col"),
        check_vma=False,
    )
```

```python
import functools
import math

import jax
import jax.numpy as jnp
from jax import lax
from jax.experimental import pallas as pl
from jax.experimental.pallas import tpu as pltpu
from jax.sharding import PartitionSpec as P

ITERS = 3
SHARPNESS = 4.0
EPSILON = 1e-06
HIGHEST = lax.Precision.HIGHEST
F32 = jnp.float32
BF16 = jnp.bfloat16
LANES = 128
STEPS = ((-1, 0), (1, 0), (0, -1), (0, 1), (-1, -1), (-1, 1), (1, -1), (1, 1))


def snake(place, rows_n):
    if rows_n % 4:
        return place
    odd_pair = lax.rem(place // 2, 2)
    return place + odd_pair * (1 - 2 * lax.rem(place, 2))


def whiten(gram):
    k = gram.shape[0]
    rows = lax.broadcasted_iota(jnp.int32, (k, k), 0)
    cols = lax.broadcasted_iota(jnp.int32, (k, k), 1)
    eye = (rows == cols).astype(F32)
    work = jnp.concatenate([gram, eye], axis=1)
    at = lax.broadcasted_iota(jnp.int32, (k, 1), 0)
    for step in range(k - 1):
        pivot = work[step : step + 1, :]
        pivot = pivot / pivot[:, step : step + 1]
        below = jnp.where(at > step, work[:, step : step + 1], 0.0)
        work = work - below * pivot
    diag = jnp.sum(work[:, :k] * eye, axis=1, keepdims=True)
    return work[:, k:] / jnp.sqrt(diag)


def kernel(
    rows_n, cols_n, th, nb, sw, scale,
    feat_ref, seq_ref, link_ref, start_ref, out_ref,
    unit, placed, land, fpad, thi, tlo, deg, vpad, grown, gsend, grecv,
    begun, linked, swapped,
    a2a_send, a2a_recv, halo_send, halo_recv, gram_send, gram_recv, swap_send, swap_recv,
    solved,
):
    row, col = lax.axis_index("row"), lax.axis_index("col")
    peers = rows_n * cols_n
    me = row * cols_n + col
    trow = snake(row, rows_n)
    moved = trow != row
    tokens, width = feat_ref.shape
    vec_n = start_ref.shape[0]
    bw = LANES
    blocks = th * nb
    chunk = th * sw
    per = LANES // chunk
    supers = tokens // LANES

    def at(peer):
        return {"row": peer // cols_n, "col": lax.rem(peer, cols_n)}

    def exists(dr, dc):
        r, c = trow + dr, col + dc
        return (r >= 0) & (r < rows_n) & (c >= 0) & (c < cols_n)

    def piece(buf, dr, dc, arriving):
        def pick(step, n):
            if step == 0:
                return pl.ds(1, n)
            if arriving:
                return pl.ds(n + 1 if step < 0 else 0, 1)
            return pl.ds(1 if step < 0 else n, 1)

        return buf.at[pick(dr, th), pick(dc, nb)]

    def halo_copy(buf, stage, way, sending):
        dr, dc = STEPS[way]
        r = snake(trow + dr if sending else trow - dr, rows_n)
        c = col + dc if sending else col - dc
        return pltpu.make_async_remote_copy(
            src_ref=piece(buf, dr, dc, False),
            dst_ref=piece(buf, dr, dc, True),
            send_sem=halo_send.at[stage, way],
            recv_sem=halo_recv.at[stage, way],
            device_id={"row": r, "col": c},
            device_id_type=pl.DeviceIdType.MESH,
        )

    def halo_start(buf, stage, ways=range(8)):
        for way in ways:
            dr, dc = STEPS[way]

            @pl.when(exists(dr, dc))
            def _():
                halo_copy(buf, stage, way, True).start()

    def halo_wait(buf, stage, ways=range(8)):
        for way in ways:
            dr, dc = STEPS[way]

            @pl.when(exists(-dr, -dc))
            def _():
                halo_copy(buf, stage, way, False).wait_recv()

    def halo_finish(buf, stage, ways=range(8)):
        for way in ways:
            dr, dc = STEPS[way]

            @pl.when(exists(dr, dc))
            def _():
                halo_copy(buf, stage, way, True).wait_send()

    def corner_copy(way):
        dr, dc = STEPS[way]
        edge = pl.ds(th + 1 if dr < 0 else 0, 1)
        return pltpu.make_async_remote_copy(
            src_ref=fpad.at[edge, pl.ds(1 if dc < 0 else nb, 1)],
            dst_ref=fpad.at[edge, pl.ds(nb + 1 if dc < 0 else 0, 1)],
            send_sem=halo_send.at[ITERS, way],
            recv_sem=halo_recv.at[ITERS, way],
            device_id={"col": col + dc},
            device_id_type=pl.DeviceIdType.MESH,
        )

    def corner_when(way, action):
        dr, dc = STEPS[way]

        @pl.when(exists(-dr, dc))
        def _():
            action(corner_copy(way))

    def swap_copy(src, dst, index):
        return pltpu.make_async_remote_copy(
            src_ref=src,
            dst_ref=dst,
            send_sem=swap_send.at[index],
            recv_sem=swap_recv.at[index],
            device_id={"row": trow},
            device_id_type=pl.DeviceIdType.MESH,
        )

    swaps = (
        (start_ref, begun, 0),
        (link_ref, linked, 1),
        (grown, swapped, 2),
    )

    def halo_zero(buf):
        for dr, dc in STEPS:
            @pl.when(jnp.logical_not(exists(-dr, -dc)))
            def _():
                where = piece(buf, dr, dc, True)
                where[...] = jnp.zeros(where.shape, where.dtype)

    barrier = pltpu.get_barrier_semaphore()

    @pl.loop(1, peers)
    def _(step):
        pl.semaphore_signal(
            barrier, inc=1, device_id=at(lax.rem(me + step, peers)),
            device_id_type=pl.DeviceIdType.MESH,
        )

    for step in range(ITERS):
        halo_zero(vpad.at[step])
    halo_zero(fpad)
    deg[...] = jnp.zeros_like(deg)

    @pl.loop(0, tokens // 64)
    def _(step):
        rows = pl.ds(pl.multiple_of(step * 64, 64), 64)
        wide = feat_ref[rows, :].astype(F32)
        squares = jnp.sum(wide * wide, axis=1, keepdims=True)
        unit[rows, :] = (wide * lax.rsqrt(squares + EPSILON)).astype(BF16)

    pl.semaphore_wait(barrier, peers - 1)

    @pl.when(moved)
    def _():
        for swap in swaps[:2]:
            swap_copy(*swap).start()

    @pl.when(jnp.logical_not(moved))
    def _():
        begun[...] = start_ref[...]
        linked[...] = link_ref[...]

    def strip_copy(index, part, dest, source):
        return pltpu.make_async_remote_copy(
            src_ref=placed.at[index, pl.ds(part * chunk, chunk)],
            dst_ref=land.at[source],
            send_sem=a2a_send.at[dest],
            recv_sem=a2a_recv.at[source],
            device_id={"row": snake(dest, rows_n)},
            device_id_type=pl.DeviceIdType.MESH,
        )

    @pl.loop(0, supers)
    def _(step):
        index = lax.rem(trow // per + supers // 2 + step, supers)
        order = seq_ref[:, pl.ds(pl.multiple_of(index * LANES, LANES), LANES)]
        order = jnp.broadcast_to(order.astype(F32), (LANES, LANES)).T
        lane = lax.broadcasted_iota(jnp.int32, (LANES, LANES), 1).astype(F32)
        chosen = jnp.concatenate(
            [
                jnp.where(order == lane + float(j * LANES), 1.0, 0.0).astype(BF16)
                for j in range(supers)
            ],
            axis=1,
        )
        placed[index] = jnp.dot(chosen, unit[...], preferred_element_type=F32).astype(BF16)
        for part in range(per):
            dest = index * per + part

            @pl.when(dest != trow)
            def _():
                strip_copy(index, part, dest, row).start()

            @pl.when(dest == trow)
            def _():
                land[row] = placed[index, pl.ds(part * chunk, chunk)]

    @pl.when(moved)
    def _():
        for swap in swaps[:2]:
            swap_copy(*swap).wait()

    for y in range(th):
        for x in range(nb):
            lo = (y * nb + x) * bw
            vpad[0, 1 + y, 1 + x] = begun[:, lo : lo + bw]
    halo_start(vpad.at[0], 0)

    group = max(1, 16 // sw)
    span = group * sw
    in_block = bw // span

    @pl.loop(0, rows_n // group)
    def _(step):
        first = lax.rem(row // group + step, rows_n // group)
        for i in range(group):
            source = first * group + i

            @pl.when(source != row)
            def _():
                strip_copy(0, 0, trow, source).wait_recv()

        rows = pl.ds(pl.multiple_of(lax.rem(first, in_block) * span, span), span)
        x = 1 + first // in_block
        if group == 1:
            for y in range(th):
                fpad[1 + y, x, rows, :] = land[first, y * sw : (y + 1) * sw, :]
        else:
            wide = [land[first * group + i].astype(F32) for i in range(group)]
            for y in range(th):
                joined = jnp.concatenate([w[y * sw : (y + 1) * sw] for w in wide], axis=0)
                fpad[1 + y, x, rows, :] = joined.astype(BF16)

    halo_start(fpad, ITERS, range(4))

    def tile(y, x, dy, dx):
        offset = (dy + 1) * 3 + dx + 1
        block = y * nb + x
        near = fpad[1 + y + dy, 1 + x + dx]
        own = fpad[1 + y, 1 + x]
        dots = lax.dot_general(
            near, own, (((1,), (1,)), ((), ())), preferred_element_type=F32
        )
        at_row, at_col = trow * th + y + dy, col * nb + x + dx
        inside = (at_row >= 0) & (at_row < rows_n * th)
        inside &= (at_col >= 0) & (at_col < cols_n * nb)
        link = jnp.where(inside, 1.0, 0.0).astype(F32)
        if offset != 4:
            link = link * linked[offset * blocks + block]
        value = jnp.exp(SHARPNESS * (dots - 1.0)) * link
        deg[block] += jnp.sum(value, axis=0, keepdims=True)
        high = value.astype(BF16)
        thi[block, offset * bw : (offset + 1) * bw, :] = high
        tlo[block, offset * bw : (offset + 1) * bw, :] = (value - high.astype(F32)).astype(BF16)

    def tiles(y, dy):
        @pl.loop(0, nb)
        def _(x):
            tile(y, x, dy, 0)

        @pl.loop(1, nb)
        def _(x):
            tile(y, x, dy, -1)
            tile(y, x - 1, dy, 1)

    def side_tiles(y, dy):
        tile(y, 0, dy, -1)
        tile(y, nb - 1, dy, 1)

    inner = [(y, dy) for y in range(th) for dy in (-1, 0, 1) if 0 <= y + dy < th]
    for y, dy in inner:
        tiles(y, dy)
    halo_wait(fpad, ITERS, (2, 3))
    for y, dy in inner:
        side_tiles(y, dy)
    edges = (((0, -1), 1, (6, 7)), ((th - 1, 1), 0, (4, 5)))
    for edge, way, corners in edges:
        halo_wait(fpad, ITERS, (way,))
        for corner in corners:
            corner_when(corner, lambda copy: copy.start())
        tiles(*edge)
    for edge, way, corners in edges:
        halo_wait(fpad, ITERS, corners)
        side_tiles(*edge)
    deg[...] = 1.0 / deg[...]

    def gram_copy(stage, dest, source):
        return pltpu.make_async_remote_copy(
            src_ref=gsend.at[stage],
            dst_ref=grecv.at[stage, source],
            send_sem=gram_send.at[stage, dest],
            recv_sem=gram_recv.at[stage, source],
            device_id=at(dest),
            device_id_type=pl.DeviceIdType.MESH,
        )

    pack = LANES // vec_n
    part_rows = vec_n // pack
    inverse = None
    for step in range(ITERS):
        halo_wait(vpad.at[step], step)
        if step > 1:
            before = inverse

            @pl.loop(0, (th + 2) * (nb + 2))
            def _(block):
                y, x = block // (nb + 2), lax.rem(block, nb + 2)
                solved[y, x] = jnp.dot(
                    before, vpad[step, y, x], precision=HIGHEST, preferred_element_type=F32
                )

        source_of = solved if step > 1 else vpad.at[step]

        @pl.loop(0, blocks)
        def _(block):
            y, x = block // nb, lax.rem(block, nb)
            field = jnp.concatenate(
                [source_of[y + o // 3, x + o % 3] for o in range(9)], axis=1
            )
            high = field.astype(BF16)
            low = (field - high.astype(F32)).astype(BF16)
            both = jnp.dot(
                jnp.concatenate([high, low], axis=0), thi[block], preferred_element_type=F32
            )
            total = both[:vec_n] + both[vec_n:]
            total += jnp.dot(high, tlo[block], preferred_element_type=F32)
            grown[:, pl.ds(pl.multiple_of(block * bw, bw), bw)] = total * deg[block]

        value = grown[...]
        if step + 1 < ITERS:
            for y in range(th):
                for x in range(nb):
                    lo = (y * nb + x) * bw
                    vpad[step + 1, 1 + y, 1 + x] = value[:, lo : lo + bw]
            halo_start(vpad.at[step + 1], step + 1)
        if step:
            total = jnp.zeros((part_rows, LANES), F32)
            last = step - 1

            def add(source, total):
                @pl.when(source != me)
                def _():
                    gram_copy(last, me, source).wait_recv()

                return total + grecv[last, source]

            total = lax.fori_loop(0, peers, add, total)
            gram = jnp.concatenate(
                [total[:, i * vec_n : (i + 1) * vec_n] for i in range(pack)], axis=0
            )
            inverse = whiten(gram)
            value = jnp.dot(inverse, value, precision=HIGHEST, preferred_element_type=F32)
            grown[...] = value
        gram = lax.dot_general(
            value, value, (((1,), (1,)), ((), ())),
            precision=HIGHEST, preferred_element_type=F32,
        )
        packed = jnp.concatenate(
            [gram[i * part_rows : (i + 1) * part_rows] for i in range(pack)], axis=1
        )
        gsend[step] = packed
        grecv[step, me] = packed

        @pl.loop(1, peers)
        def _(other):
            gram_copy(step, lax.rem(me + other, peers), me).start()

        if step + 1 == ITERS:
            @pl.when(moved)
            def _():
                swap_copy(*swaps[2]).start()

            @pl.when(jnp.logical_not(moved))
            def _():
                swapped[...] = value

    def add(source, total):
        @pl.when(source != me)
        def _():
            gram_copy(ITERS - 1, me, source).wait_recv()

        return total + grecv[ITERS - 1, source]

    total = lax.fori_loop(0, peers, add, jnp.zeros((part_rows, LANES), F32))
    gram = jnp.concatenate(
        [total[:, i * vec_n : (i + 1) * vec_n] for i in range(pack)], axis=0
    )
    inverse = whiten(gram)

    @pl.when(moved)
    def _():
        swap_copy(*swaps[2]).wait()

    out_ref[...] = jnp.dot(
        inverse, swapped[...], precision=HIGHEST, preferred_element_type=F32
    ) * scale

    for step in range(ITERS):
        halo_finish(vpad.at[step], step)

        @pl.loop(1, peers)
        def _(other):
            gram_copy(step, lax.rem(me + other, peers), me).wait_send()

    halo_finish(fpad, ITERS, range(4))
    for way in range(4, 8):
        corner_when(way, lambda copy: copy.wait_send())

    @pl.loop(0, rows_n)
    def _(dest):
        @pl.when(dest != trow)
        def _():
            strip_copy(0, 0, dest, row).wait_send()


def body(features, seq_order, block_links, start_vectors):
    rows_n = lax.axis_size("row")
    cols_n = lax.axis_size("col")
    tokens, width = features.shape
    vec_n, th, tile_w = start_vectors.shape
    nb = block_links.shape[2]
    sw = tile_w // rows_n
    bw = tile_w // nb
    peers = rows_n * cols_n
    blocks = th * nb
    scale = math.sqrt(th * rows_n * tile_w * cols_n)
    part_rows = vec_n * vec_n // LANES
    links = (block_links == 1).astype(F32).reshape(9 * blocks, 1, 1)
    links = jnp.broadcast_to(links, (9 * blocks, 1, LANES))
    vmem = pl.BlockSpec(memory_space=pltpu.VMEM)
    dma = pltpu.SemaphoreType.DMA
    out = pl.pallas_call(
        functools.partial(kernel, rows_n, cols_n, th, nb, sw, scale),
        out_shape=jax.ShapeDtypeStruct((vec_n, tokens), F32),
        in_specs=[vmem] * 4,
        out_specs=vmem,
        scratch_shapes=[
            pltpu.VMEM((tokens, width), BF16),
            pltpu.VMEM((tokens // LANES, LANES, width), BF16),
            pltpu.VMEM((rows_n, th * sw, width), BF16),
            pltpu.VMEM((th + 2, nb + 2, bw, width), BF16),
            pltpu.VMEM((blocks, 9 * bw, bw), BF16),
            pltpu.VMEM((blocks, 9 * bw, bw), BF16),
            pltpu.VMEM((blocks, 1, bw), F32),
            pltpu.VMEM((ITERS, th + 2, nb + 2, vec_n, bw), F32),
            pltpu.VMEM((vec_n, tokens), F32),
            pltpu.VMEM((ITERS, part_rows, LANES), F32),
            pltpu.VMEM((ITERS, peers, part_rows, LANES), F32),
            pltpu.VMEM((vec_n, tokens), F32),
            pltpu.VMEM((9 * blocks, 1, LANES), F32),
            pltpu.VMEM((vec_n, tokens), F32),
            dma((rows_n,)),
            dma((rows_n,)),
            dma((ITERS + 1, len(STEPS))),
            dma((ITERS + 1, len(STEPS))),
            dma((ITERS, peers)),
            dma((ITERS, peers)),
            dma((3,)),
            dma((3,)),
            pltpu.VMEM((th + 2, nb + 2, vec_n, bw), F32),
        ],
        compiler_params=pltpu.CompilerParams(
            collective_id=0, has_side_effects=True, vmem_limit_bytes=48 * 2**20
        ),
    )(features, seq_order, links, start_vectors.reshape(vec_n, tokens))
    return out.reshape(vec_n, th, tile_w)


def solution(mesh):
    return jax.shard_map(
        body,
        mesh=mesh,
        in_specs=(
            P(("slide", "row", "col"), None),
            P(("slide", "row", "col"), None),
            P(None, ("slide", "row"), "col"),
            P(None, ("slide", "row"), "col"),
        ),
        out_specs=P(None, ("slide", "row"), "col"),
        check_vma=False,
    )
```
